32 devices in a mesh: ctx: 16 (over z, y, core), chan: 2 (over x).
Axes of the slice: x: 2, y: 2, z: 4, core: 2. Of those that a mesh axis runs over, the one named last changes fastest.
Arguments:
- sequence: bfloat16 [2048, 4096], P('ctx', 'chan'), may hold values from -6 to 6
- in_weight: bfloat16 [3, 4096, 2048], P(None, 'ctx', 'chan'), may hold values from -0.09375 to 0.09375
- short_taps: float32 [3, 7, 2048], P(None, None, 'chan'), may hold values from -2 to 2
- decay_rates: float32 [128, 16], P('chan'), may hold values from 0.00012207031 to 0.03
- residues: float32 [128, 16], P('chan'), may hold values from -1.5 to 1.5
- skip_gain: float32 [2048], P('chan'), may hold values from -5 to 5
Outputs:
- mixed: bfloat16 [2048, 2048], P('ctx', 'chan')
The draws below stay inside these ranges and needn't reach their ends.
All inputs are finite; a program needn't handle non-finite values.
Results may differ from the reference program's by a relative error of at most 0.0064.
Values may be sent and summed in bfloat16 or wider, within the bound.
A program may use at most 64 MiB of HBM per device.

```python
import math
import jax
import jax.numpy as jnp
from jax import lax

D = 4096
CHANNELS = 2048
FGROUP = 16
ORDER = 16
TAPS = 7
TOKENS = 2048
FFTLEN = 4096
FILTERS = 128


def block_levels(own_key, shape, cuts, low, high):
    gain = 1.0
    for axis_at, blocks in cuts:
        steps = jax.random.uniform(jax.random.fold_in(jax.random.fold_in(own_key, 6), axis_at), (blocks,), jnp.float32, low / len(cuts), high / len(cuts))
        gain = gain * jnp.repeat(jnp.exp(steps), shape[axis_at] // blocks).reshape((-1,) + (1,) * (len(shape) - 1 - axis_at))
    return gain


def noise(stream_key, extent, scale, most, shards=(), kind=jnp.bfloat16):
    array = scale * jax.random.normal(stream_key, extent, jnp.float32)
    if shards:
        array = array * block_levels(stream_key, extent, shards, -0.22, 0.18)
    return jnp.clip(array, -most, most).astype(kind)


def setup_inputs(seed: int = 0) -> dict:
    streams_of = jax.random.split(jax.random.key(seed), 7)
    sequence = noise(streams_of[0], (TOKENS, D), 1.0, 6.0, ((0, 16), (1, 2)))
    in_weight = noise(streams_of[1], (3, D, CHANNELS), D ** -0.5, 0.09375, ((1, 16), (2, 2)))
    short_taps = noise(streams_of[2], (3, TAPS, CHANNELS), TAPS ** -0.5, 2.0, ((2, 2),), jnp.float32)
    decay_rates = jnp.clip(jnp.exp(math.log(0.03) - 5.5043554 * jax.random.uniform(streams_of[3], (FILTERS, ORDER), jnp.float32) ** block_levels(streams_of[3], (FILTERS, ORDER), ((0, 2),), -0.2, 0.2)), 0.00012207031, 0.03)
    residues = noise(streams_of[4], (FILTERS, ORDER), 0.25, 1.5, ((0, 2),), jnp.float32)
    skip_gain = noise(streams_of[5], (CHANNELS,), 1.0, 5.0, ((0, 2),), jnp.float32)
    return {"sequence": sequence, "in_weight": in_weight, "short_taps": short_taps, "decay_rates": decay_rates, "residues": residues, "skip_gain": skip_gain}


def reference(sequence, in_weight, short_taps, decay_rates, residues, skip_gain):
    projections = jnp.stack([jnp.dot(sequence, in_weight[slot], preferred_element_type=jnp.float32) for slot in range(3)]).astype(jnp.bfloat16)
    padded = jnp.pad(projections, ((0, 0), (TAPS - 1, 0), (0, 0)))
    filtered = jnp.zeros((3, TOKENS, CHANNELS), jnp.float32)
    for tap in range(TAPS):
        window = padded[:, TAPS - 1 - tap:TAPS - 1 - tap + TOKENS, :].astype(jnp.float32)
        filtered = filtered + short_taps[:, tap, None, :] * window
    query = filtered[0]
    signal = filtered[1] * filtered[2]
    moments = jnp.arange(TOKENS, dtype=jnp.float32)
    weights = residues * jnp.sqrt(2.0 * decay_rates)
    impulse = jnp.zeros((FILTERS, TOKENS), jnp.float32)
    for mode in range(ORDER):
        impulse = impulse + weights[:, mode, None] * jnp.exp(-decay_rates[:, mode, None] * moments[None, :])
    blocks = jnp.transpose(signal.reshape(TOKENS, FILTERS, FGROUP), (1, 0, 2))

    def convolve(pair):
        block, kernel = pair
        spectrum = jnp.fft.rfft(block, n=FFTLEN, axis=0) * jnp.fft.rfft(kernel, n=FFTLEN)[:, None]
        return jnp.fft.irfft(spectrum, n=FFTLEN, axis=0)[:TOKENS]
    conv = lax.map(convolve, (blocks, impulse))
    conv = jnp.transpose(conv, (1, 0, 2)).reshape(TOKENS, CHANNELS)
    return (query * (conv + skip_gain * signal)).astype(jnp.bfloat16)
```

```python
import functools
import math

import jax
import jax.numpy as jnp
from jax import lax
from jax.experimental import pallas as pl
from jax.experimental.pallas import tpu as pltpu
from jax.sharding import PartitionSpec as P

FGROUP = 16
CHUNK = 128


HIGHEST = lax.Precision.HIGHEST


def shifted(block, axis, distance):
    devices = range(lax.axis_size(axis))
    route = [(i - distance, i) for i in devices if i - distance in devices]
    return lax.ppermute(block, axis, route)


def rotation(numerator, period):
    angle = -2.0 * math.pi / period * numerator.astype(jnp.float32)
    return (jnp.cos(angle), jnp.sin(angle))


def complex_times(real_part, imag_part, cosine, sine):
    return (real_part * cosine - imag_part * sine, real_part * sine + imag_part * cosine)


def rotate_field(field, cosine, sine):
    real_part, imag_part = complex_times(field[0], field[1], cosine, sine)
    return jnp.stack([real_part, imag_part])


def open_padding(real_part, imag_part, offsets, fft_length):
    cosine, sine = rotation(offsets, fft_length)
    turned_real, turned_imag = complex_times(real_part, imag_part, cosine[:, None], sine[:, None])
    return jnp.stack([jnp.stack([real_part, turned_real]), jnp.stack([imag_part, turned_imag])])


def close_padding(field, offsets, fft_length):
    cosine, sine = rotation(offsets, fft_length)
    turned_real, turned_imag = complex_times(
        field[0, 1], field[1, 1], cosine[:, None], -sine[:, None]
    )
    return ((field[0, 0] + turned_real) / fft_length, (field[1, 0] + turned_imag) / fft_length)


def dft_table(length, sign):
    indices = jnp.arange(length, dtype=jnp.int32)
    products = indices[:, None] * indices[None, :] % length
    angle = sign * 2.0 * math.pi / length * products.astype(jnp.float32)
    return (jnp.cos(angle), jnp.sin(angle))


def apply_table(table, field):
    cosine, sine = table
    real_out = jnp.einsum("kp,hpqw->hkqw", cosine, field[0], precision=HIGHEST) - jnp.einsum(
        "kp,hpqw->hkqw", sine, field[1], precision=HIGHEST
    )
    imag_out = jnp.einsum("kp,hpqw->hkqw", cosine, field[1], precision=HIGHEST) + jnp.einsum(
        "kp,hpqw->hkqw", sine, field[0], precision=HIGHEST
    )
    return jnp.stack([real_out, imag_out])


def middle_rotation(field, device_pos, count, quarter, seq_length, sign):
    columns = device_pos * quarter + jnp.arange(quarter, dtype=jnp.int32)
    cosine, sine = rotation(
        jnp.arange(count, dtype=jnp.int32)[:, None] * columns[None, :] % seq_length, seq_length
    )
    return rotate_field(field, cosine[:, :, None], sign * sine[:, :, None])


def apply_response(spectrum, response, group_pairs):
    shape = spectrum.shape
    grouped = spectrum.reshape(shape[0], shape[1], shape[2], response.shape[3], group_pairs)
    real_part, imag_part = complex_times(
        grouped[0], grouped[1], response[0][..., None], response[1][..., None]
    )
    return jnp.stack([real_part, imag_part]).reshape(shape)


def spread_positions(sequence, in_weight, short_taps, decay_rates, residues, skip_gain):
    whole = lax.all_gather(sequence, "chan", axis=1, tiled=True)
    row_count = whole.shape[0]
    lane_count = in_weight.shape[2]
    projections = jnp.einsum(
        "td,sdc->stc",
        whole,
        lax.all_gather(in_weight, "ctx", axis=1, tiled=True),
        preferred_element_type=jnp.float32,
    ).astype(jnp.bfloat16)
    tap_count = short_taps.shape[1]
    edge = shifted(projections[:, row_count - (tap_count - 1) :, :], "ctx", 1)
    extended = jnp.concatenate([edge, projections], axis=1)
    filtered = jnp.zeros((3, row_count, lane_count), jnp.float32)
    for tap_index in range(tap_count):
        begin = tap_count - 1 - tap_index
        filtered = filtered + short_taps[:, tap_index, None, :] * extended[
            :, begin : begin + row_count, :
        ].astype(jnp.float32)
    query = filtered[0]
    signal = filtered[1] * filtered[2]
    device_pos = lax.axis_index("ctx")
    count = lax.axis_size("ctx")
    seq_length = row_count * count
    fft_length = 2 * seq_length
    offsets = device_pos * row_count + jnp.arange(row_count, dtype=jnp.int32)
    moments = offsets.astype(jnp.float32)
    mode_weights = residues * jnp.sqrt(2.0 * decay_rates)
    impulse = jnp.sum(
        mode_weights[None, :, :] * jnp.exp(-decay_rates[None, :, :] * moments[:, None, None]),
        axis=2,
    )
    paired = signal.reshape(row_count, lane_count // 2, 2)
    spectrum = open_padding(paired[:, :, 0], paired[:, :, 1], offsets, fft_length)
    response = open_padding(impulse, jnp.zeros_like(impulse), offsets, fft_length)
    quarter = row_count // count
    across_forward = dft_table(count, -1.0)
    within_forward = dft_table(row_count, -1.0)
    across_back = dft_table(count, 1.0)
    within_back = dft_table(row_count, 1.0)
    moved_signal, moved_response = (
        lax.all_to_all(spectrum[:, :, None], "ctx", split_axis=3, concat_axis=2, tiled=True),
        lax.all_to_all(response[:, :, None], "ctx", split_axis=3, concat_axis=2, tiled=True),
    )
    moved_signal = middle_rotation(
        apply_table(across_forward, moved_signal), device_pos, count, quarter, seq_length, 1.0
    )
    moved_response = middle_rotation(
        apply_table(across_forward, moved_response), device_pos, count, quarter, seq_length, 1.0
    )
    spread_signal, spread_response = (
        lax.all_to_all(moved_signal, "ctx", split_axis=2, concat_axis=3, tiled=True),
        lax.all_to_all(moved_response, "ctx", split_axis=2, concat_axis=3, tiled=True),
    )
    spectrum = apply_table(within_forward, spread_signal[:, :, 0][:, :, :, None])[:, :, :, 0]
    response = apply_table(within_forward, spread_response[:, :, 0][:, :, :, None])[:, :, :, 0]
    product = apply_response(spectrum, response, FGROUP // 2)
    returned = apply_table(within_back, product[:, :, :, None])[:, :, :, 0]
    returned = lax.all_to_all(returned[:, :, None], "ctx", split_axis=3, concat_axis=2, tiled=True)
    returned = apply_table(
        across_back, middle_rotation(returned, device_pos, count, quarter, seq_length, -1.0)
    )
    returned = lax.all_to_all(returned, "ctx", split_axis=2, concat_axis=3, tiled=True)
    product = returned[:, :, 0]
    conv_real, conv_imag = close_padding(product, offsets, fft_length)
    conv = jnp.stack([conv_real, conv_imag], axis=2).reshape(row_count, lane_count)
    return (query * (conv + skip_gain * signal)).astype(jnp.bfloat16)


def operator_kernel(groups, proj_ref, taps_ref, skip_ref, near_ref, into_ref, out_of_ref, decay_ref, mixed_ref):
    total = proj_ref.shape[2]
    chunks = total // CHUNK
    tap_count = taps_ref.shape[2]
    lane = lax.broadcasted_iota(jnp.int32, (FGROUP, total), 1)
    for group in range(groups):
        rows = pl.ds(group * FGROUP, FGROUP)
        streams = []
        for slot in range(3):
            block = proj_ref[slot, rows, :].astype(jnp.float32)
            taps = taps_ref[slot, rows, :]
            filtered = taps[:, 0:1] * block
            for tap in range(1, tap_count):
                moved = jnp.where(lane >= tap, pltpu.roll(block, tap, 1), 0.0)
                filtered = filtered + taps[:, tap : tap + 1] * moved
            streams.append(filtered)
        query, key, value = streams
        signal = key * value
        stacked = jnp.concatenate(
            [signal[:, a * CHUNK : (a + 1) * CHUNK] for a in range(chunks)], axis=0
        )
        near = jnp.dot(stacked, near_ref[group], precision=HIGHEST)
        added = jnp.dot(stacked, into_ref[group], precision=HIGHEST)
        decay = decay_ref[group]
        state = jnp.zeros((FGROUP, added.shape[1]), jnp.float32)
        states = []
        for a in range(chunks):
            states.append(state)
            state = state * decay + added[a * FGROUP : (a + 1) * FGROUP, :]
        far = jnp.dot(jnp.concatenate(states, axis=0), out_of_ref[group], precision=HIGHEST)
        out = near + far
        conv = jnp.concatenate(
            [out[a * FGROUP : (a + 1) * FGROUP, :] for a in range(chunks)], axis=1
        )
        mixed = query * (conv + skip_ref[rows, :] * signal)
        mixed_ref[rows, :] = mixed.astype(mixed_ref.dtype)


def filter_tables(decay_rates, residues):
    steps = jnp.arange(CHUNK, dtype=jnp.int32)
    moments = steps.astype(jnp.float32)
    weights = residues * jnp.sqrt(2.0 * decay_rates)
    lag = steps[None, :] - steps[:, None]
    near = jnp.sum(
        weights[:, :, None, None]
        * jnp.exp(-decay_rates[:, :, None, None] * jnp.maximum(lag, 0).astype(jnp.float32)),
        axis=1,
    )
    near = jnp.where(lag >= 0, near, 0.0)
    into = jnp.exp(-decay_rates[:, None, :] * (CHUNK - 1.0 - moments)[None, :, None])
    out_of = weights[:, :, None] * jnp.exp(-decay_rates[:, :, None] * (moments + 1.0))
    decay = jnp.exp(-decay_rates * float(CHUNK))[:, None, :]
    return near, into, out_of, decay


def own_part(array, size, axis):
    return lax.dynamic_slice_in_dim(array, lax.axis_index("ctx") * size, size, axis)


def spread_channels(sequence, in_weight, short_taps, decay_rates, residues, skip_gain):
    count = lax.axis_size("ctx")
    halves = lax.axis_size("chan")
    own_rows, features = sequence.shape
    slots, own_depth, lanes = in_weight.shape
    total = own_rows * count
    own = lanes // count
    groups = own // FGROUP
    gathered = lax.all_gather(sequence, ("chan", "ctx"), axis=0, tiled=True)
    gathered = gathered.reshape(halves, total, features)
    parts = in_weight.reshape(slots, own_depth, count, own).transpose(2, 0, 3, 1)
    parts = lax.all_to_all(parts, "ctx", split_axis=0, concat_axis=0, tiled=True)
    weight = parts.transpose(1, 2, 0, 3).reshape(slots * own, halves, features)
    tables = filter_tables(
        own_part(decay_rates, groups, 0), own_part(residues, groups, 0)
    )
    taps = own_part(short_taps, own, 2).transpose(0, 2, 1)
    skip = own_part(skip_gain, own, 0)[:, None]
    projections = jnp.einsum(
        "nhd,htd->nt", weight, gathered, preferred_element_type=jnp.float32
    ).astype(jnp.bfloat16)
    mixed = pl.pallas_call(
        functools.partial(operator_kernel, groups),
        out_shape=jax.ShapeDtypeStruct((own, total), jnp.bfloat16),
        compiler_params=pltpu.CompilerParams(vmem_limit_bytes=32 * 2**20),
        name="operator",
    )(projections.reshape(slots, own, total), taps, skip, *tables)
    mixed = lax.all_to_all(mixed, "ctx", split_axis=1, concat_axis=0, tiled=True)
    return mixed.T


def per_device(sequence, in_weight, short_taps, decay_rates, residues, skip_gain):
    count = lax.axis_size("ctx")
    halves = lax.axis_size("chan")
    sequence_bytes = sequence.size * count * halves
    weight_bytes = in_weight.size * count
    own = in_weight.shape[2] // count
    by_channel = (
        sequence_bytes <= weight_bytes
        and own % FGROUP == 0
        and sequence.shape[0] * count % CHUNK == 0
    )
    plan = spread_channels if by_channel else spread_positions
    return plan(sequence, in_weight, short_taps, decay_rates, residues, skip_gain)


def solution(mesh):
    return jax.shard_map(
        per_device,
        mesh=mesh,
        in_specs=(
            P("ctx", "chan"),
            P(None, "ctx", "chan"),
            P(None, None, "chan"),
            P("chan", None),
            P("chan", None),
            P("chan"),
        ),
        out_specs=P("ctx", "chan"),
        check_vma=False,
    )
```

```python
import functools
import math

import jax
import jax.numpy as jnp
from jax import lax
from jax.experimental import pallas as pl
from jax.experimental.pallas import tpu as pltpu
from jax.sharding import PartitionSpec as P

FGROUP = 16
CHUNK = 128


HIGHEST = lax.Precision.HIGHEST


def shifted(block, axis, distance):
    devices = range(lax.axis_size(axis))
    route = [(i - distance, i) for i in devices if i - distance in devices]
    return lax.ppermute(block, axis, route)


def rotation(numerator, period):
    angle = -2.0 * math.pi / period * numerator.astype(jnp.float32)
    return (jnp.cos(angle), jnp.sin(angle))


def complex_times(real_part, imag_part, cosine, sine):
    return (real_part * cosine - imag_part * sine, real_part * sine + imag_part * cosine)


def rotate_field(field, cosine, sine):
    real_part, imag_part = complex_times(field[0], field[1], cosine, sine)
    return jnp.stack([real_part, imag_part])


def open_padding(real_part, imag_part, offsets, fft_length):
    cosine, sine = rotation(offsets, fft_length)
    turned_real, turned_imag = complex_times(real_part, imag_part, cosine[:, None], sine[:, None])
    return jnp.stack([jnp.stack([real_part, turned_real]), jnp.stack([imag_part, turned_imag])])


def close_padding(field, offsets, fft_length):
    cosine, sine = rotation(offsets, fft_length)
    turned_real, turned_imag = complex_times(
        field[0, 1], field[1, 1], cosine[:, None], -sine[:, None]
    )
    return ((field[0, 0] + turned_real) / fft_length, (field[1, 0] + turned_imag) / fft_length)


def dft_table(length, sign):
    indices = jnp.arange(length, dtype=jnp.int32)
    products = indices[:, None] * indices[None, :] % length
    angle = sign * 2.0 * math.pi / length * products.astype(jnp.float32)
    return (jnp.cos(angle), jnp.sin(angle))


def apply_table(table, field):
    cosine, sine = table
    real_out = jnp.einsum("kp,hpqw->hkqw", cosine, field[0], precision=HIGHEST) - jnp.einsum(
        "kp,hpqw->hkqw", sine, field[1], precision=HIGHEST
    )
    imag_out = jnp.einsum("kp,hpqw->hkqw", cosine, field[1], precision=HIGHEST) + jnp.einsum(
        "kp,hpqw->hkqw", sine, field[0], precision=HIGHEST
    )
    return jnp.stack([real_out, imag_out])


def middle_rotation(field, device_pos, count, quarter, seq_length, sign):
    columns = device_pos * quarter + jnp.arange(quarter, dtype=jnp.int32)
    cosine, sine = rotation(
        jnp.arange(count, dtype=jnp.int32)[:, None] * columns[None, :] % seq_length, seq_length
    )
    return rotate_field(field, cosine[:, :, None], sign * sine[:, :, None])


def apply_response(spectrum, response, group_pairs):
    shape = spectrum.shape
    grouped = spectrum.reshape(shape[0], shape[1], shape[2], response.shape[3], group_pairs)
    real_part, imag_part = complex_times(
        grouped[0], grouped[1], response[0][..., None], response[1][..., None]
    )
    return jnp.stack([real_part, imag_part]).reshape(shape)


def spread_positions(sequence, in_weight, short_taps, decay_rates, residues, skip_gain):
    whole = lax.all_gather(sequence, "chan", axis=1, tiled=True)
    row_count = whole.shape[0]
    lane_count = in_weight.shape[2]
    projections = jnp.einsum(
        "td,sdc->stc",
        whole,
        lax.all_gather(in_weight, "ctx", axis=1, tiled=True),
        preferred_element_type=jnp.float32,
    ).astype(jnp.bfloat16)
    tap_count = short_taps.shape[1]
    edge = shifted(projections[:, row_count - (tap_count - 1) :, :], "ctx", 1)
    extended = jnp.concatenate([edge, projections], axis=1)
    filtered = jnp.zeros((3, row_count, lane_count), jnp.float32)
    for tap_index in range(tap_count):
        begin = tap_count - 1 - tap_index
        filtered = filtered + short_taps[:, tap_index, None, :] * extended[
            :, begin : begin + row_count, :
        ].astype(jnp.float32)
    query = filtered[0]
    signal = filtered[1] * filtered[2]
    device_pos = lax.axis_index("ctx")
    count = lax.axis_size("ctx")
    seq_length = row_count * count
    fft_length = 2 * seq_length
    offsets = device_pos * row_count + jnp.arange(row_count, dtype=jnp.int32)
    moments = offsets.astype(jnp.float32)
    mode_weights = residues * jnp.sqrt(2.0 * decay_rates)
    impulse = jnp.sum(
        mode_weights[None, :, :] * jnp.exp(-decay_rates[None, :, :] * moments[:, None, None]),
        axis=2,
    )
    paired = signal.reshape(row_count, lane_count // 2, 2)
    spectrum = open_padding(paired[:, :, 0], paired[:, :, 1], offsets, fft_length)
    response = open_padding(impulse, jnp.zeros_like(impulse), offsets, fft_length)
    quarter = row_count // count
    across_forward = dft_table(count, -1.0)
    within_forward = dft_table(row_count, -1.0)
    across_back = dft_table(count, 1.0)
    within_back = dft_table(row_count, 1.0)
    moved_signal, moved_response = (
        lax.all_to_all(spectrum[:, :, None], "ctx", split_axis=3, concat_axis=2, tiled=True),
        lax.all_to_all(response[:, :, None], "ctx", split_axis=3, concat_axis=2, tiled=True),
    )
    moved_signal = middle_rotation(
        apply_table(across_forward, moved_signal), device_pos, count, quarter, seq_length, 1.0
    )
    moved_response = middle_rotation(
        apply_table(across_forward, moved_response), device_pos, count, quarter, seq_length, 1.0
    )
    spread_signal, spread_response = (
        lax.all_to_all(moved_signal, "ctx", split_axis=2, concat_axis=3, tiled=True),
        lax.all_to_all(moved_response, "ctx", split_axis=2, concat_axis=3, tiled=True),
    )
    spectrum = apply_table(within_forward, spread_signal[:, :, 0][:, :, :, None])[:, :, :, 0]
    response = apply_table(within_forward, spread_response[:, :, 0][:, :, :, None])[:, :, :, 0]
    product = apply_response(spectrum, response, FGROUP // 2)
    returned = apply_table(within_back, product[:, :, :, None])[:, :, :, 0]
    returned = lax.all_to_all(returned[:, :, None], "ctx", split_axis=3, concat_axis=2, tiled=True)
    returned = apply_table(
        across_back, middle_rotation(returned, device_pos, count, quarter, seq_length, -1.0)
    )
    returned = lax.all_to_all(returned, "ctx", split_axis=2, concat_axis=3, tiled=True)
    product = returned[:, :, 0]
    conv_real, conv_imag = close_padding(product, offsets, fft_length)
    conv = jnp.stack([conv_real, conv_imag], axis=2).reshape(row_count, lane_count)
    return (query * (conv + skip_gain * signal)).astype(jnp.bfloat16)


def operator_kernel(groups, proj_ref, taps_ref, skip_ref, near_ref, into_ref, out_of_ref, decay_ref, mixed_ref):
    total = proj_ref.shape[2]
    chunks = total // CHUNK
    tap_count = taps_ref.shape[2]
    lane = lax.broadcasted_iota(jnp.int32, (FGROUP, total), 1)
    for group in range(groups):
        rows = pl.ds(group * FGROUP, FGROUP)
        streams = []
        for slot in range(3):
            block = proj_ref[slot, rows, :].astype(jnp.float32)
            taps = taps_ref[slot, rows, :]
            filtered = taps[:, 0:1] * block
            for tap in range(1, tap_count):
                moved = jnp.where(lane >= tap, pltpu.roll(block, tap, 1), 0.0)
                filtered = filtered + taps[:, tap : tap + 1] * moved
            streams.append(filtered)
        query, key, value = streams
        signal = key * value
        stacked = jnp.concatenate(
            [signal[:, a * CHUNK : (a + 1) * CHUNK] for a in range(chunks)], axis=0
        )
        near = jnp.dot(stacked, near_ref[group], precision=HIGHEST)
        added = jnp.dot(stacked, into_ref[group], precision=HIGHEST)
        decay = decay_ref[group]
        state = jnp.zeros((FGROUP, added.shape[1]), jnp.float32)
        states = []
        for a in range(chunks):
            states.append(state)
            state = state * decay + added[a * FGROUP : (a + 1) * FGROUP, :]
        far = jnp.dot(jnp.concatenate(states, axis=0), out_of_ref[group], precision=HIGHEST)
        out = near + far
        conv = jnp.concatenate(
            [out[a * FGROUP : (a + 1) * FGROUP, :] for a in range(chunks)], axis=1
        )
        mixed = query * (conv + skip_ref[rows, :] * signal)
        mixed_ref[rows, :] = mixed.astype(mixed_ref.dtype)


MESH = pl.DeviceIdType.MESH
PIECE = 32
CORES = 2
SIDE = 2


def gather_kernel(count, seq_ref, parts_ref, proj_ref, held, weight, w_send, w_recv, send, recv):
    me = lax.axis_index("ctx")
    x = lax.axis_index("chan")
    core = me % CORES
    y = me // CORES % SIDE
    z = me // (CORES * SIDE)
    depth_z = count // (CORES * SIDE)
    rows = seq_ref.shape[0]
    pieces = rows // PIECE
    depth = parts_ref.shape[2]
    per_half = count // 2

    def ctx_of(zz, yy, cc):
        return (zz * SIDE + yy) * CORES + cc

    barrier = pltpu.get_barrier_semaphore()

    def greet(step, carry):
        pl.semaphore_signal(
            barrier, inc=1, device_id=((me + step) % count, x), device_id_type=MESH
        )
        return carry

    lax.fori_loop(1, count, greet, 0)
    pl.semaphore_signal(barrier, inc=1, device_id=(me, 1 - x), device_id_type=MESH)
    pl.semaphore_wait(barrier, count)

    def weight_copy(part, source, target):
        lanes = pl.ds(pl.multiple_of(source % per_half * depth, depth), depth)
        return pltpu.make_async_remote_copy(
            src_ref=parts_ref.at[part],
            dst_ref=weight.at[source // per_half, :, lanes],
            send_sem=w_send.at[part],
            recv_sem=w_recv.at[source],
            device_id=(target, x),
            device_id_type=MESH,
        )

    def piece_copy(xx, block, piece, kind, target):
        where = held.at[xx, pl.ds(pl.multiple_of(block * rows + piece * PIECE, PIECE), PIECE), :]
        return pltpu.make_async_remote_copy(
            src_ref=where,
            dst_ref=where,
            send_sem=send.at[kind, xx, block, piece],
            recv_sem=recv.at[xx, block, piece],
            device_id=target,
            device_id_type=MESH,
        )

    def first_hop(piece):
        late = piece // (pieces - 1)
        return (1 - late) * (1 - y) + late * y, (1 - late) * x + late * (1 - x)

    def second_hop(piece):
        late = piece // (pieces - 1)
        return late * (1 - y) + (1 - late) * y, late * x + (1 - late) * (1 - x)

    sibling = (ctx_of(z, y, 1 - core), x)

    def valid(d):
        return (z + d >= 0) & (z + d < depth_z)

    def send_on(d, piece, act):
        block = ctx_of(z + d, y, core)
        if d >= 0:
            @pl.when(z > 0)
            def _():
                act(piece_copy(x, block, piece, 0, (ctx_of(z - 1, y, core), x)))
        if d <= 0:
            @pl.when(z < depth_z - 1)
            def _():
                act(piece_copy(x, block, piece, 1, (ctx_of(z + 1, y, core), x)))
        yy, xx = first_hop(piece)
        act(piece_copy(x, block, piece, 2, (ctx_of(z, yy, core), xx)))
        yy, xx = second_hop(piece)
        act(piece_copy(x, block, piece, 3, (ctx_of(z, yy, core), xx)))
        act(piece_copy(x, block, piece, 4, sibling))

    def send_turned(d, piece, act):
        yy, xx = first_hop(piece)
        block = ctx_of(z + d, yy, core)
        y2, x2 = second_hop(piece)
        act(piece_copy(xx, block, piece, 3, (ctx_of(z, y2, core), x2)))
        act(piece_copy(xx, block, piece, 4, sibling))

    def send_last(d, piece, act):
        y2, x2 = second_hop(piece)
        act(piece_copy(x2, ctx_of(z + d, y2, core), piece, 4, sibling))
        act(piece_copy(1 - x, ctx_of(z + d, 1 - y, core), piece, 4, sibling))

    def arrived(xx, block, piece):
        piece_copy(xx, block, piece, 4, sibling).wait_recv()

    def each_piece(d, body):
        @pl.when(valid(d))
        def _():
            def step(piece, carry):
                body(piece)
                return carry
            lax.fori_loop(0, pieces, step, 0)

    def start(copy):
        copy.start()

    def finish(copy):
        copy.wait_send()

    def stage_line(d):
        def body(piece):
            if d != 0:
                arrived(x, ctx_of(z + d, y, core), piece)
            send_on(d, piece, start)
        each_piece(d, body)

    def stage_turned(d):
        def body(piece):
            yy, xx = first_hop(piece)
            arrived(xx, ctx_of(z + d, yy, core), piece)
            send_turned(d, piece, start)
        each_piece(d, body)

    def stage_last(d):
        def body(piece):
            y2, x2 = second_hop(piece)
            arrived(x2, ctx_of(z + d, y2, core), piece)
            arrived(1 - x, ctx_of(z + d, 1 - y, core), piece)
            send_last(d, piece, start)
        each_piece(d, body)

    def multiply(d):
        def body(piece):
            for yy in range(SIDE):
                for xx in range(2):
                    arrived(xx, ctx_of(z + d, yy, 1 - core), piece)
        each_piece(d, body)

        @pl.when(valid(d))
        def _():
            width = CORES * rows
            def step(yy, carry):
                span = pl.ds(pl.multiple_of(ctx_of(z + d, yy, 0) * rows, width), width)
                out = jnp.zeros((weight.shape[1], width), jnp.float32)
                for xx in range(2):
                    out = out + lax.dot_general(
                        weight[xx], held[xx, span, :], (((1,), (1,)), ((), ())),
                        preferred_element_type=jnp.float32,
                    )
                proj_ref[:, span] = out.astype(proj_ref.dtype)
                return carry
            lax.fori_loop(0, SIDE, step, 0)

    held[x, pl.ds(pl.multiple_of(me * rows, rows), rows), :] = seq_ref[...]
    stage_line(0)

    def send_weight(step, carry):
        target = (me + step) % count
        weight_copy(target, me, target).start()
        return carry

    lax.fori_loop(1, count, send_weight, 0)
    own = pl.ds(pl.multiple_of(me % per_half * depth, depth), depth)
    weight[me // per_half, :, own] = parts_ref[me]

    order = [0]
    for far in range(1, depth_z):
        order += [far, -far]
    for d in order[1:3]:
        stage_line(d)
    stage_turned(order[0])
    for d in order[3:5]:
        stage_line(d)
    for d in order[1:3]:
        stage_turned(d)
    stage_last(order[0])
    for d in order[5:]:
        stage_line(d)
    for d in order[3:5]:
        stage_turned(d)
    for d in order[1:3]:
        stage_last(d)
    for d in order[5:]:
        stage_turned(d)

    def take_weight(step, carry):
        source = (me + step) % count
        weight_copy(source, source, source).wait_recv()
        return carry

    lax.fori_loop(1, count, take_weight, 0)
    for d in order[3:5]:
        stage_last(d)
    for d in order[:3]:
        multiply(d)
    for d in order[5:]:
        stage_last(d)
    for d in order[3:]:
        multiply(d)

    def sent_weight(step, carry):
        target = (me + step) % count
        weight_copy(target, me, target).wait_send()
        return carry

    lax.fori_loop(1, count, sent_weight, 0)
    for d in order:
        each_piece(d, lambda piece: send_on(d, piece, finish))
        each_piece(d, lambda piece: send_turned(d, piece, finish))
        each_piece(d, lambda piece: send_last(d, piece, finish))


def gather_project(sequence, parts, count):
    rows, features = sequence.shape
    own, depth = parts.shape[1:]
    pieces = rows // PIECE
    return pl.pallas_call(
        functools.partial(gather_kernel, count),
        out_shape=jax.ShapeDtypeStruct((own, rows * count), jnp.bfloat16),
        in_specs=[pl.BlockSpec(memory_space=pltpu.VMEM)] * 2,
        out_specs=pl.BlockSpec(memory_space=pltpu.VMEM),
        scratch_shapes=[
            pltpu.VMEM((2, count * rows, features), jnp.bfloat16),
            pltpu.VMEM((2, own, features), jnp.bfloat16),
            pltpu.SemaphoreType.DMA((count,)),
            pltpu.SemaphoreType.DMA((count,)),
            pltpu.SemaphoreType.DMA((5, 2, count, pieces)),
            pltpu.SemaphoreType.DMA((2, count, pieces)),
        ],
        compiler_params=pltpu.CompilerParams(
            collective_id=0, has_side_effects=True, vmem_limit_bytes=40 * 2**20
        ),
        name="gather_project",
    )(sequence, parts)


def filter_tables(decay_rates, residues):
    steps = jnp.arange(CHUNK, dtype=jnp.int32)
    moments = steps.astype(jnp.float32)
    weights = residues * jnp.sqrt(2.0 * decay_rates)
    lag = steps[None, :] - steps[:, None]
    near = jnp.sum(
        weights[:, :, None, None]
        * jnp.exp(-decay_rates[:, :, None, None] * jnp.maximum(lag, 0).astype(jnp.float32)),
        axis=1,
    )
    near = jnp.where(lag >= 0, near, 0.0)
    into = jnp.exp(-decay_rates[:, None, :] * (CHUNK - 1.0 - moments)[None, :, None])
    out_of = weights[:, :, None] * jnp.exp(-decay_rates[:, :, None] * (moments + 1.0))
    decay = jnp.exp(-decay_rates * float(CHUNK))[:, None, :]
    return near, into, out_of, decay


def own_part(array, size, axis):
    return lax.dynamic_slice_in_dim(array, lax.axis_index("ctx") * size, size, axis)


def spread_channels(sequence, in_weight, short_taps, decay_rates, residues, skip_gain):
    count = lax.axis_size("ctx")
    own_rows, features = sequence.shape
    slots, own_depth, lanes = in_weight.shape
    total = own_rows * count
    own = lanes // count
    groups = own // FGROUP
    parts = in_weight.reshape(slots, own_depth, count, own).transpose(2, 0, 3, 1)
    parts = parts.reshape(count, slots * own, own_depth)
    tables = filter_tables(
        own_part(decay_rates, groups, 0), own_part(residues, groups, 0)
    )
    taps = own_part(short_taps, own, 2).transpose(0, 2, 1)
    skip = own_part(skip_gain, own, 0)[:, None]
    projections = gather_project(sequence, parts, count)
    mixed = pl.pallas_call(
        functools.partial(operator_kernel, groups),
        out_shape=jax.ShapeDtypeStruct((own, total), jnp.bfloat16),
        compiler_params=pltpu.CompilerParams(vmem_limit_bytes=32 * 2**20),
        name="operator",
    )(projections.reshape(slots, own, total), taps, skip, *tables)
    mixed = lax.all_to_all(mixed, "ctx", split_axis=1, concat_axis=0, tiled=True)
    return mixed.T


def per_device(sequence, in_weight, short_taps, decay_rates, residues, skip_gain):
    count = lax.axis_size("ctx")
    halves = lax.axis_size("chan")
    sequence_bytes = sequence.size * count * halves
    weight_bytes = in_weight.size * count
    own = in_weight.shape[2] // count
    by_channel = (
        sequence_bytes <= weight_bytes
        and own % FGROUP == 0
        and halves == 2
        and count % (CORES * SIDE * 2) == 0
        and sequence.shape[0] % (2 * PIECE) == 0
        and in_weight.shape[1] * count == sequence.shape[1] * halves
        and sequence.shape[0] * count % CHUNK == 0
    )
    plan = spread_channels if by_channel else spread_positions
    return plan(sequence, in_weight, short_taps, decay_rates, residues, skip_gain)


def solution(mesh):
    return jax.shard_map(
        per_device,
        mesh=mesh,
        in_specs=(
            P("ctx", "chan"),
            P(None, "ctx", "chan"),
            P(None, None, "chan"),
            P("chan", None),
            P("chan", None),
            P("chan"),
        ),
        out_specs=P("ctx", "chan"),
        check_vma=False,
    )
```

```python
import functools
import math

import jax
import jax.numpy as jnp
from jax import lax
from jax.experimental import pallas as pl
from jax.experimental.pallas import tpu as pltpu
from jax.sharding import PartitionSpec as P

FGROUP = 16
CHUNK = 128


HIGHEST = lax.Precision.HIGHEST


def shifted(block, axis, distance):
    devices = range(lax.axis_size(axis))
    route = [(i - distance, i) for i in devices if i - distance in devices]
    return lax.ppermute(block, axis, route)


def rotation(numerator, period):
    angle = -2.0 * math.pi / period * numerator.astype(jnp.float32)
    return (jnp.cos(angle), jnp.sin(angle))


def complex_times(real_part, imag_part, cosine, sine):
    return (real_part * cosine - imag_part * sine, real_part * sine + imag_part * cosine)


def rotate_field(field, cosine, sine):
    real_part, imag_part = complex_times(field[0], field[1], cosine, sine)
    return jnp.stack([real_part, imag_part])


def open_padding(real_part, imag_part, offsets, fft_length):
    cosine, sine = rotation(offsets, fft_length)
    turned_real, turned_imag = complex_times(real_part, imag_part, cosine[:, None], sine[:, None])
    return jnp.stack([jnp.stack([real_part, turned_real]), jnp.stack([imag_part, turned_imag])])


def close_padding(field, offsets, fft_length):
    cosine, sine = rotation(offsets, fft_length)
    turned_real, turned_imag = complex_times(
        field[0, 1], field[1, 1], cosine[:, None], -sine[:, None]
    )
    return ((field[0, 0] + turned_real) / fft_length, (field[1, 0] + turned_imag) / fft_length)


def dft_table(length, sign):
    indices = jnp.arange(length, dtype=jnp.int32)
    products = indices[:, None] * indices[None, :] % length
    angle = sign * 2.0 * math.pi / length * products.astype(jnp.float32)
    return (jnp.cos(angle), jnp.sin(angle))


def apply_table(table, field):
    cosine, sine = table
    real_out = jnp.einsum("kp,hpqw->hkqw", cosine, field[0], precision=HIGHEST) - jnp.einsum(
        "kp,hpqw->hkqw", sine, field[1], precision=HIGHEST
    )
    imag_out = jnp.einsum("kp,hpqw->hkqw", cosine, field[1], precision=HIGHEST) + jnp.einsum(
        "kp,hpqw->hkqw", sine, field[0], precision=HIGHEST
    )
    return jnp.stack([real_out, imag_out])


def middle_rotation(field, device_pos, count, quarter, seq_length, sign):
    columns = device_pos * quarter + jnp.arange(quarter, dtype=jnp.int32)
    cosine, sine = rotation(
        jnp.arange(count, dtype=jnp.int32)[:, None] * columns[None, :] % seq_length, seq_length
    )
    return rotate_field(field, cosine[:, :, None], sign * sine[:, :, None])


def apply_response(spectrum, response, group_pairs):
    shape = spectrum.shape
    grouped = spectrum.reshape(shape[0], shape[1], shape[2], response.shape[3], group_pairs)
    real_part, imag_part = complex_times(
        grouped[0], grouped[1], response[0][..., None], response[1][..., None]
    )
    return jnp.stack([real_part, imag_part]).reshape(shape)


def spread_positions(sequence, in_weight, short_taps, decay_rates, residues, skip_gain):
    whole = lax.all_gather(sequence, "chan", axis=1, tiled=True)
    row_count = whole.shape[0]
    lane_count = in_weight.shape[2]
    projections = jnp.einsum(
        "td,sdc->stc",
        whole,
        lax.all_gather(in_weight, "ctx", axis=1, tiled=True),
        preferred_element_type=jnp.float32,
    ).astype(jnp.bfloat16)
    tap_count = short_taps.shape[1]
    edge = shifted(projections[:, row_count - (tap_count - 1) :, :], "ctx", 1)
    extended = jnp.concatenate([edge, projections], axis=1)
    filtered = jnp.zeros((3, row_count, lane_count), jnp.float32)
    for tap_index in range(tap_count):
        begin = tap_count - 1 - tap_index
        filtered = filtered + short_taps[:, tap_index, None, :] * extended[
            :, begin : begin + row_count, :
        ].astype(jnp.float32)
    query = filtered[0]
    signal = filtered[1] * filtered[2]
    device_pos = lax.axis_index("ctx")
    count = lax.axis_size("ctx")
    seq_length = row_count * count
    fft_length = 2 * seq_length
    offsets = device_pos * row_count + jnp.arange(row_count, dtype=jnp.int32)
    moments = offsets.astype(jnp.float32)
    mode_weights = residues * jnp.sqrt(2.0 * decay_rates)
    impulse = jnp.sum(
        mode_weights[None, :, :] * jnp.exp(-decay_rates[None, :, :] * moments[:, None, None]),
        axis=2,
    )
    paired = signal.reshape(row_count, lane_count // 2, 2)
    spectrum = open_padding(paired[:, :, 0], paired[:, :, 1], offsets, fft_length)
    response = open_padding(impulse, jnp.zeros_like(impulse), offsets, fft_length)
    quarter = row_count // count
    across_forward = dft_table(count, -1.0)
    within_forward = dft_table(row_count, -1.0)
    across_back = dft_table(count, 1.0)
    within_back = dft_table(row_count, 1.0)
    moved_signal, moved_response = (
        lax.all_to_all(spectrum[:, :, None], "ctx", split_axis=3, concat_axis=2, tiled=True),
        lax.all_to_all(response[:, :, None], "ctx", split_axis=3, concat_axis=2, tiled=True),
    )
    moved_signal = middle_rotation(
        apply_table(across_forward, moved_signal), device_pos, count, quarter, seq_length, 1.0
    )
    moved_response = middle_rotation(
        apply_table(across_forward, moved_response), device_pos, count, quarter, seq_length, 1.0
    )
    spread_signal, spread_response = (
        lax.all_to_all(moved_signal, "ctx", split_axis=2, concat_axis=3, tiled=True),
        lax.all_to_all(moved_response, "ctx", split_axis=2, concat_axis=3, tiled=True),
    )
    spectrum = apply_table(within_forward, spread_signal[:, :, 0][:, :, :, None])[:, :, :, 0]
    response = apply_table(within_forward, spread_response[:, :, 0][:, :, :, None])[:, :, :, 0]
    product = apply_response(spectrum, response, FGROUP // 2)
    returned = apply_table(within_back, product[:, :, :, None])[:, :, :, 0]
    returned = lax.all_to_all(returned[:, :, None], "ctx", split_axis=3, concat_axis=2, tiled=True)
    returned = apply_table(
        across_back, middle_rotation(returned, device_pos, count, quarter, seq_length, -1.0)
    )
    returned = lax.all_to_all(returned, "ctx", split_axis=2, concat_axis=3, tiled=True)
    product = returned[:, :, 0]
    conv_real, conv_imag = close_padding(product, offsets, fft_length)
    conv = jnp.stack([conv_real, conv_imag], axis=2).reshape(row_count, lane_count)
    return (query * (conv + skip_gain * signal)).astype(jnp.bfloat16)


def operate(groups, sums, taps_ref, skip_ref, near_ref, into_ref, out_of_ref, decay_ref, mixed_ref):
    own, total = mixed_ref.shape
    chunks = total // CHUNK
    tap_count = taps_ref.shape[2]
    lane = lax.broadcasted_iota(jnp.int32, (FGROUP, total), 1)
    for group in range(groups):
        rows = pl.ds(group * FGROUP, FGROUP)
        streams = []
        for slot in range(3):
            block = sums[pl.ds(slot * own + group * FGROUP, FGROUP), :]
            block = block.astype(jnp.bfloat16).astype(jnp.float32)
            taps = taps_ref[slot, rows, :]
            filtered = taps[:, 0:1] * block
            for tap in range(1, tap_count):
                moved = jnp.where(lane >= tap, pltpu.roll(block, tap, 1), 0.0)
                filtered = filtered + taps[:, tap : tap + 1] * moved
            streams.append(filtered)
        query, key, value = streams
        signal = key * value
        stacked = jnp.concatenate(
            [signal[:, a * CHUNK : (a + 1) * CHUNK] for a in range(chunks)], axis=0
        )
        near = jnp.dot(stacked, near_ref[group], precision=HIGHEST)
        added = jnp.dot(stacked, into_ref[group], precision=HIGHEST)
        decay = decay_ref[group]
        state = jnp.zeros((FGROUP, added.shape[1]), jnp.float32)
        states = []
        for a in range(chunks):
            states.append(state)
            state = state * decay + added[a * FGROUP : (a + 1) * FGROUP, :]
        far = jnp.dot(jnp.concatenate(states, axis=0), out_of_ref[group], precision=HIGHEST)
        out = near + far
        conv = jnp.concatenate(
            [out[a * FGROUP : (a + 1) * FGROUP, :] for a in range(chunks)], axis=1
        )
        mixed = query * (conv + skip_ref[rows, :] * signal)
        mixed_ref[rows, :] = mixed.astype(mixed_ref.dtype)


MESH = pl.DeviceIdType.MESH
PIECE = 32
CORES = 2
SIDE = 2


def gather_kernel(
    count, groups, seq_ref, parts_ref, taps_ref, skip_ref, near_ref, into_ref, out_of_ref, decay_ref,
    out_ref, held, weight, kept, given, taken, mixed,
    w_send, w_recv, send, recv, p_send, p_recv, o_send, o_recv,
):
    me = lax.axis_index("ctx")
    x = lax.axis_index("chan")
    core = me % CORES
    y = me // CORES % SIDE
    z = me // (CORES * SIDE)
    depth_z = count // (CORES * SIDE)
    rows = seq_ref.shape[0]
    pieces = rows // PIECE
    own, depth = parts_ref.shape[1:]
    per_half = count // 2
    width = CORES * rows
    half = me // per_half

    def ctx_of(zz, yy, cc):
        return (zz * SIDE + yy) * CORES + cc

    barrier = pltpu.get_barrier_semaphore()

    def greet(step, carry):
        target = (me + step) % count
        pl.semaphore_signal(barrier, inc=1, device_id=(target, x), device_id_type=MESH)
        pl.semaphore_signal(barrier, inc=1, device_id=(target, 1 - x), device_id_type=MESH)
        return carry

    lax.fori_loop(1, count, greet, 0)
    pl.semaphore_signal(barrier, inc=1, device_id=(me, 1 - x), device_id_type=MESH)
    pl.semaphore_wait(barrier, 2 * count - 1)

    def weight_copy(part, source, column, target):
        lanes = pl.ds(pl.multiple_of(source % per_half * depth, depth), depth)
        return pltpu.make_async_remote_copy(
            src_ref=parts_ref.at[part],
            dst_ref=weight.at[column, :, lanes],
            send_sem=w_send.at[part],
            recv_sem=w_recv.at[column, source % per_half],
            device_id=target,
            device_id_type=MESH,
        )

    def each_target(act):
        def step(index, carry):
            target = (me + index) % count
            act(weight_copy(target, me, x, (target, half)))
            return carry

        lax.fori_loop(1, count, step, 0)

        @pl.when(half != x)
        def _():
            act(weight_copy(me, me, x, (me, half)))

    def piece_copy(block, piece, kind, target):
        where = held.at[pl.ds(pl.multiple_of(block * rows + piece * PIECE, PIECE), PIECE), :]
        return pltpu.make_async_remote_copy(
            src_ref=where,
            dst_ref=where,
            send_sem=send.at[kind, block, piece],
            recv_sem=recv.at[block, piece],
            device_id=(target, x),
            device_id_type=MESH,
        )

    sibling = ctx_of(z, y, 1 - core)

    def valid(d):
        return (z + d >= 0) & (z + d < depth_z)

    def send_on(d, piece, act):
        block = ctx_of(z + d, y, core)
        if d >= 0:
            @pl.when(z > 0)
            def _():
                act(piece_copy(block, piece, 0, ctx_of(z - 1, y, core)))
        if d <= 0:
            @pl.when(z < depth_z - 1)
            def _():
                act(piece_copy(block, piece, 1, ctx_of(z + 1, y, core)))
        act(piece_copy(block, piece, 2, ctx_of(z, 1 - y, core)))
        act(piece_copy(block, piece, 3, sibling))

    def send_turned(d, piece, act):
        act(piece_copy(ctx_of(z + d, 1 - y, core), piece, 3, sibling))

    def arrived(block, piece):
        piece_copy(block, piece, 3, sibling).wait_recv()

    def each_piece(d, body):
        @pl.when(valid(d))
        def _():
            def step(piece, carry):
                body(piece)
                return carry

            lax.fori_loop(0, pieces, step, 0)

    def start(copy):
        copy.start()

    def finish(copy):
        copy.wait_send()

    def stage_line(d):
        def body(piece):
            if d != 0:
                arrived(ctx_of(z + d, y, core), piece)
            send_on(d, piece, start)

        each_piece(d, body)

    def stage_turned(d):
        def body(piece):
            arrived(ctx_of(z + d, 1 - y, core), piece)
            send_turned(d, piece, start)

        each_piece(d, body)

    def columns(pair):
        return pl.ds(pl.multiple_of(pair * width, width), width)

    def partial_copy(pair):
        return pltpu.make_async_remote_copy(
            src_ref=given.at[:, columns(pair)],
            dst_ref=taken.at[:, columns(pair)],
            send_sem=p_send.at[pair],
            recv_sem=p_recv.at[pair],
            device_id=(me, 1 - x),
            device_id_type=MESH,
        )

    def multiply(d, side):
        yy = y if side == 0 else 1 - y
        each_piece(d, lambda piece: arrived(ctx_of(z + d, yy, 1 - core), piece))

        @pl.when(valid(d))
        def _():
            pair = (z + d) * SIDE + yy
            block = held[columns(pair), :]
            for column, into in ((1 - x, given), (x, kept)):
                into[:, columns(pair)] = lax.dot_general(
                    weight[column], block, (((1,), (1,)), ((), ())),
                    preferred_element_type=jnp.float32,
                )
                if into is given:
                    partial_copy(pair).start()

    held[pl.ds(pl.multiple_of(me * rows, rows), rows), :] = seq_ref[...]
    stage_line(0)
    each_target(start)

    @pl.when(half == x)
    def _():
        lanes = pl.ds(pl.multiple_of(me % per_half * depth, depth), depth)
        weight[x, :, lanes] = parts_ref[me]

    order = [0]
    for far in range(1, depth_z):
        order += [far, -far]
    for d in order[1:3]:
        stage_line(d)
    stage_turned(order[0])
    for d in order[3:5]:
        stage_line(d)
    for d in order[1:3]:
        stage_turned(d)
    for d in order[5:]:
        stage_line(d)
    for d in order[3:5]:
        stage_turned(d)

    def take_weight(step, carry):
        source = x * per_half + step % per_half
        column = step // per_half

        @pl.when((source != me) | (column != x))
        def _():
            weight_copy(source, source, column, (me, 1 - x)).wait_recv()

        return carry

    lax.fori_loop(0, count, take_weight, 0)
    for d in order[:3]:
        multiply(d, 0)
    for d in order[:3]:
        multiply(d, 1)
    for d in order[3:5]:
        multiply(d, 0)
    for d in order[5:]:
        stage_turned(d)
    for d in order[3:5]:
        multiply(d, 1)
    for d in order[5:]:
        multiply(d, 0)
        multiply(d, 1)

    def join(pair, carry):
        partial_copy(pair).wait_recv()
        kept[:, columns(pair)] = kept[:, columns(pair)] + taken[:, columns(pair)]
        return carry

    lax.fori_loop(0, count // CORES, join, 0)
    operate(groups, kept, taps_ref, skip_ref, near_ref, into_ref, out_of_ref, decay_ref, mixed)
    lanes = mixed.shape[0]

    def out_copy(part, source, target):
        return pltpu.make_async_remote_copy(
            src_ref=mixed.at[:, pl.ds(pl.multiple_of(part * rows, rows), rows)],
            dst_ref=out_ref.at[pl.ds(pl.multiple_of(source * lanes, lanes), lanes), :],
            send_sem=o_send.at[part],
            recv_sem=o_recv.at[source],
            device_id=(target, x),
            device_id_type=MESH,
        )

    def send_out(step, carry):
        target = (me + step) % count
        out_copy(target, me, target).start()
        return carry

    lax.fori_loop(1, count, send_out, 0)
    out_ref[pl.ds(pl.multiple_of(me * lanes, lanes), lanes), :] = mixed[
        :, pl.ds(pl.multiple_of(me * rows, rows), rows)
    ]

    each_target(finish)
    for d in order:
        each_piece(d, lambda piece: send_on(d, piece, finish))
        each_piece(d, lambda piece: send_turned(d, piece, finish))

    def finish_partial(pair, carry):
        partial_copy(pair).wait_send()
        return carry

    lax.fori_loop(0, count // CORES, finish_partial, 0)

    def finish_out(step, carry):
        other = (me + step) % count
        out_copy(other, other, other).wait()
        return carry

    lax.fori_loop(1, count, finish_out, 0)


def gather_operate(sequence, parts, taps, skip, tables, count, groups):
    rows, features = sequence.shape
    own, depth = parts.shape[1:]
    lanes = own // 3
    pieces = rows // PIECE
    total = rows * count
    inputs = (sequence, parts, taps, skip, *tables)
    return pl.pallas_call(
        functools.partial(gather_kernel, count, groups),
        out_shape=jax.ShapeDtypeStruct((lanes * count, rows), jnp.bfloat16),
        in_specs=[pl.BlockSpec(memory_space=pltpu.VMEM)] * len(inputs),
        out_specs=pl.BlockSpec(memory_space=pltpu.VMEM),
        scratch_shapes=[
            pltpu.VMEM((total, features), jnp.bfloat16),
            pltpu.VMEM((2, own, features), jnp.bfloat16),
            pltpu.VMEM((own, total), jnp.float32),
            pltpu.VMEM((own, total), jnp.float32),
            pltpu.VMEM((own, total), jnp.float32),
            pltpu.VMEM((lanes, total), jnp.bfloat16),
            pltpu.SemaphoreType.DMA((count,)),
            pltpu.SemaphoreType.DMA((2, count // 2)),
            pltpu.SemaphoreType.DMA((4, count, pieces)),
            pltpu.SemaphoreType.DMA((count, pieces)),
            pltpu.SemaphoreType.DMA((count // CORES,)),
            pltpu.SemaphoreType.DMA((count // CORES,)),
            pltpu.SemaphoreType.DMA((count,)),
            pltpu.SemaphoreType.DMA((count,)),
        ],
        compiler_params=pltpu.CompilerParams(
            collective_id=0, has_side_effects=True, vmem_limit_bytes=40 * 2**20
        ),
        name="gather_operate",
    )(*inputs)


def filter_tables(decay_rates, residues):
    steps = jnp.arange(CHUNK, dtype=jnp.int32)
    moments = steps.astype(jnp.float32)
    weights = residues * jnp.sqrt(2.0 * decay_rates)
    lag = steps[None, :] - steps[:, None]
    near = jnp.sum(
        weights[:, :, None, None]
        * jnp.exp(-decay_rates[:, :, None, None] * jnp.maximum(lag, 0).astype(jnp.float32)),
        axis=1,
    )
    near = jnp.where(lag >= 0, near, 0.0)
    into = jnp.exp(-decay_rates[:, None, :] * (CHUNK - 1.0 - moments)[None, :, None])
    out_of = weights[:, :, None] * jnp.exp(-decay_rates[:, :, None] * (moments + 1.0))
    decay = jnp.exp(-decay_rates * float(CHUNK))[:, None, :]
    return near, into, out_of, decay


def own_part(array, size, axis):
    return lax.dynamic_slice_in_dim(array, lax.axis_index("ctx") * size, size, axis)


def spread_channels(sequence, in_weight, short_taps, decay_rates, residues, skip_gain):
    count = lax.axis_size("ctx")
    own_rows, features = sequence.shape
    slots, own_depth, lanes = in_weight.shape
    total = own_rows * count
    own = lanes // count
    groups = own // FGROUP
    parts = in_weight.reshape(slots, own_depth, count, own).transpose(2, 0, 3, 1)
    parts = parts.reshape(count, slots * own, own_depth)
    tables = filter_tables(
        own_part(decay_rates, groups, 0), own_part(residues, groups, 0)
    )
    taps = own_part(short_taps, own, 2).transpose(0, 2, 1)
    skip = own_part(skip_gain, own, 0)[:, None]
    mixed = gather_operate(sequence, parts, taps, skip, tables, count, groups)
    return mixed.T


def per_device(sequence, in_weight, short_taps, decay_rates, residues, skip_gain):
    count = lax.axis_size("ctx")
    halves = lax.axis_size("chan")
    sequence_bytes = sequence.size * count * halves
    weight_bytes = in_weight.size * count
    own = in_weight.shape[2] // count
    by_channel = (
        sequence_bytes <= weight_bytes
        and own % FGROUP == 0
        and halves == 2
        and count % (CORES * SIDE * 2) == 0
        and sequence.shape[0] % (2 * PIECE) == 0
        and in_weight.shape[1] * count == sequence.shape[1] * halves
        and sequence.shape[0] * count % CHUNK == 0
    )
    plan = spread_channels if by_channel else spread_positions
    return plan(sequence, in_weight, short_taps, decay_rates, residues, skip_gain)


def solution(mesh):
    return jax.shard_map(
        per_device,
        mesh=mesh,
        in_specs=(
            P("ctx", "chan"),
            P(None, "ctx", "chan"),
            P(None, None, "chan"),
            P("chan", None),
            P("chan", None),
            P("chan"),
        ),
        out_specs=P("ctx", "chan"),
        check_vma=False,
    )
```
